32 devices in a mesh: dp: 2 (over core), seq: 16 (over z, y, x).
Axes of the slice: x: 2, y: 2, z: 4, core: 2. Of those that a mesh axis runs over, the one named last changes fastest.
Arguments:
- query: bfloat16 [2, 8192, 1536], P('dp', 'seq'), may hold values from -6 to 6
- key: bfloat16 [2, 8192, 1536], P('dp', 'seq'), may hold values from -6 to 6
- value: bfloat16 [2, 8192, 1536], P('dp', 'seq'), may hold values from -6 to 6
- block_weights: bfloat16 [64, 128, 128], P('seq', 'dp'), may hold values from -0.5 to 0.5
- mix_weights: bfloat16 [128, 64, 64], P('seq', 'dp'), may hold values from -1.5 to 1.5
- block_index: int32 [64, 16], replicated, may hold values from 0 to 63, all different within a row
- cotangent: bfloat16 [2, 8192, 1536], P('dp', 'seq'), may hold values from -6 to 6
Outputs:
- output: bfloat16 [2, 8192, 1536], P('dp', 'seq')
- grad_query: bfloat16 [2, 8192, 1536], P('dp', 'seq')
- grad_key: bfloat16 [2, 8192, 1536], P('dp', 'seq')
- grad_value: bfloat16 [2, 8192, 1536], P('dp', 'seq')
- grad_blocks: float32 [64, 128, 128], P('seq', 'dp')
- grad_mix: float32 [128, 64, 64], P('seq', 'dp')
The draws below stay inside these ranges and needn't reach their ends.
Inputs may be any that keep to these rules, and one draw needn't show every extreme that they name: `block_index`: each row names 16 different blocks, and every block is named by some row.
All inputs are finite; a program needn't handle non-finite values.
Results may differ from the reference program's by a relative error of at most 0.0064.
Values may be sent and summed in bfloat16 or wider, within the bound.
A program may use at most 64 MiB of HBM per device.

```python
import jax
import jax.numpy as jnp
from jax import lax

CHANNEL_WIDTH = 1536
BS = 128
NNZ = 16
BATCH = 2
SEQUENCE_LENGTH = 8192
NB = 64


def level_of(rng, shape, split, smallest, high):
    loudness, own = 1.0, jax.random.fold_in(rng, 6)
    for dim, shards_of in split:
        steps = jnp.exp(jax.random.uniform(jax.random.fold_in(own, dim), (shards_of,), jnp.float32, smallest / len(split), high / len(split)))
        loudness = loudness * jnp.repeat(steps, shape[dim] // shards_of).reshape([-1 if axis == dim else 1 for axis in range(len(shape))])
    return loudness


def picks_of(key, rows, count, top, lift):
    ranking = jax.random.permutation(jax.random.fold_in(key, 1), count)
    pull = ranking
    for power in range(3):
        pull = pull * pull // count
    pull = pull * lift // count
    chance = jax.random.randint(jax.random.fold_in(key, 2), (rows, count), 0, 4096) + pull
    sure = jax.random.permutation(jax.random.fold_in(key, 3), rows)[jnp.arange(count) % rows]
    chance = jnp.where(jnp.arange(rows)[:, None] == sure[None, :], 1 << 14, chance)
    merit = chance * count + jnp.arange(count)
    return lax.top_k(merit.astype(jnp.int32), top)[1].astype(jnp.int32)


def bell_draw(stream_key, shape, spread, most, shards=(), kind=jnp.bfloat16):
    factor_of = level_of(stream_key, shape, shards, -0.22, 0.18) if shards else 1.0
    values = jax.random.normal(stream_key, shape, jnp.float32) * spread * factor_of
    return jnp.minimum(jnp.maximum(values, -most), most).astype(kind)


def setup_inputs(seed: int = 0) -> dict:
    keys = jax.random.split(jax.random.key(seed), 8)
    return {
        "query": bell_draw(keys[0], (BATCH, SEQUENCE_LENGTH, CHANNEL_WIDTH), 1.0, 6.0, ((0, 2), (1, 16))),
        "key": bell_draw(keys[1], (BATCH, SEQUENCE_LENGTH, CHANNEL_WIDTH), 1.0, 6.0, ((0, 2), (1, 16))),
        "value": bell_draw(keys[2], (BATCH, SEQUENCE_LENGTH, CHANNEL_WIDTH), 1.0, 6.0, ((0, 2), (1, 16))),
        "block_weights": bell_draw(keys[3], (NB, BS, BS), BS ** -0.5, 0.5, ((0, 16), (1, 2))),
        "mix_weights": bell_draw(keys[4], (BS, NB, NB), NNZ ** -0.5, 1.5, ((0, 16), (1, 2))),
        "block_index": picks_of(keys[5], NB, NB, NNZ, 0),
        "cotangent": bell_draw(keys[6], (BATCH, SEQUENCE_LENGTH, CHANNEL_WIDTH), 1.0, 6.0, ((0, 2), (1, 16))),
    }


def rounded_value(values):
    return lax.optimization_barrier(values.astype(jnp.bfloat16)).astype(jnp.float32)


def block_mask(block_index):
    columns = jnp.arange(NB, dtype=jnp.int32)
    hits = (block_index[:, :, None] == columns[None, None, :]).astype(jnp.float32)
    return jnp.max(hits, axis=1)


def reference(query, key, value, block_weights, mix_weights, block_index, cotangent):
    pattern = block_mask(block_index)
    masked = mix_weights.astype(jnp.float32) * pattern[None]
    block_tiles = block_weights.astype(jnp.float32)

    def sample(items):
        query_row, key_row, value_row, cot_row = items
        query_f = query_row.astype(jnp.float32)
        key_f = key_row.astype(jnp.float32)
        value_f = value_row.astype(jnp.float32)
        cot_f = cot_row.astype(jnp.float32)
        split_parts = rounded_value(key_f * value_f).reshape(NB, BS, CHANNEL_WIDTH)
        first_factor = rounded_value(jnp.einsum("nfq,nql->nfl", block_tiles, split_parts))
        mixed = rounded_value(jnp.einsum("jik,kjd->ijd", masked, first_factor)).reshape(SEQUENCE_LENGTH, CHANNEL_WIDTH)
        output = (query_f * mixed).astype(jnp.bfloat16)
        grad_query = (cot_f * mixed).astype(jnp.bfloat16)
        grad_mixed = rounded_value(cot_f * query_f).reshape(NB, BS, CHANNEL_WIDTH)
        first_factor_gradient = rounded_value(jnp.einsum("jik,ijd->kjd", masked, grad_mixed))
        mix_term = jnp.einsum("ijd,kjd->jik", grad_mixed, first_factor) * pattern[None]
        product_gradient = jnp.einsum("obj,obv->ojv", block_tiles, first_factor_gradient).reshape(SEQUENCE_LENGTH, CHANNEL_WIDTH)
        grad_key = (product_gradient * value_f).astype(jnp.bfloat16)
        grad_value = (product_gradient * key_f).astype(jnp.bfloat16)
        sparse_block_part = jnp.einsum("ejo,eso->ejs", first_factor_gradient, split_parts)
        return output, grad_query, grad_key, grad_value, sparse_block_part, mix_term

    results = lax.map(sample, (query, key, value, cotangent))
    return (results[0], results[1], results[2], results[3],
            jnp.sum(results[4], axis=0), jnp.sum(results[5], axis=0))
```

```python
import functools

import jax
import jax.numpy as jnp
from jax import lax
from jax.experimental import pallas as pl
from jax.experimental.pallas import tpu as pltpu
from jax.sharding import PartitionSpec as P

F32 = jnp.float32
BF16 = jnp.bfloat16
G, F, H, M = range(4)


def log2(x):
    return x.bit_length() - 1


def iota(shape, dim):
    return lax.broadcasted_iota(jnp.int32, shape, dim)


def onehot(cond):
    return jnp.where(cond, 1.0, 0.0).astype(BF16)


def dot(a, b):
    return jnp.dot(a, b, preferred_element_type=F32)


def dot_nt(a, b):
    return lax.dot_general(a, b, (((1,), (1,)), ((), ())), preferred_element_type=F32)


def dot_tn(a, b):
    return lax.dot_general(a, b, (((0,), (0,)), ((), ())), preferred_element_type=F32)


def thirds(x):
    hi = x.astype(BF16)
    rest = x - hi.astype(F32)
    mid = rest.astype(BF16)
    return hi, mid, (rest - mid.astype(F32)).astype(BF16)


def kernel(
    n, ndp, tile,
    q_ref, k_ref, v_ref, c_ref, w_ref, mx_ref, bi_ref,
    o_ref, gq_ref, gk_ref, gv_ref, gb_ref, gm_ref,
    gs, gr, fs, fr, hs, hr, ms, mr,
    prod, gfn, bmat, btm, wfull, wg, mg, pr, gms, gmr, gbs, gbr,
    send, recv, dsend, drecv, lsem, wsem,
):
    rows, width = q_ref.shape
    blocks, bs = w_ref.shape[0], w_ref.shape[2]
    nb, nnz = bi_ref.shape
    offs = bs // n
    chunk = blocks * offs
    own = nb // ndp
    part = own * offs
    a_loc = w_ref.shape[1]
    me = lax.axis_index("seq")
    core = lax.axis_index("dp")

    def peer(i):
        return lax.rem(me + 1 + lax.rem(n // 2 - 1 + 4 * i, n - 1), n)

    def mate(i):
        return lax.rem(core + 1 + i, ndp)

    barrier = pltpu.get_barrier_semaphore()

    @pl.loop(0, n - 1)
    def _(i):
        pl.semaphore_signal(
            barrier, inc=1, device_id={"dp": core, "seq": lax.rem(me + 1 + i, n)},
            device_id_type=pl.DeviceIdType.MESH,
        )

    @pl.loop(0, ndp - 1)
    def _(i):
        pl.semaphore_signal(
            barrier, inc=1, device_id={"dp": mate(i), "seq": me},
            device_id_type=pl.DeviceIdType.MESH,
        )

    pl.semaphore_wait(barrier, n + ndp - 2)

    def across(kind, src, dst, to, slot):
        return pltpu.make_async_remote_copy(
            src_ref=src.at[to], dst_ref=dst.at[slot],
            send_sem=send.at[kind, to], recv_sem=recv.at[kind, slot],
            device_id={"dp": core, "seq": to}, device_id_type=pl.DeviceIdType.MESH,
        )

    def exchange(kind, src, dst):
        @pl.loop(0, n - 1)
        def _(i):
            across(kind, src, dst, peer(i), me).start()

        pltpu.make_async_copy(src.at[me], dst.at[me], lsem.at[kind]).start()

    def arrived(kind, src, dst):
        @pl.loop(0, n - 1)
        def _(i):
            across(kind, src, dst, me, peer(i)).wait_recv()

        pltpu.make_async_copy(src.at[me], dst.at[me], lsem.at[kind]).wait()

    def left(kind, src, dst):
        @pl.loop(0, n - 1)
        def _(i):
            across(kind, src, dst, peer(i), me).wait_send()

    def beside(kind, src, dst, to, slot):
        return pltpu.make_async_remote_copy(
            src_ref=src, dst_ref=dst.at[slot],
            send_sem=dsend.at[kind, to], recv_sem=drecv.at[kind, slot],
            device_id={"dp": to, "seq": me}, device_id_type=pl.DeviceIdType.MESH,
        )

    def columns(body):
        @pl.loop(0, width // tile)
        def _(t):
            body(pl.ds(pl.multiple_of(t * tile, tile), tile))

    def place(shape, row_dim):
        r = iota(shape, row_dim)
        rem = r & (chunk - 1)
        return (rem >> log2(offs)) * bs + (r >> log2(chunk)) * offs + (rem & (offs - 1))

    def to_chunks(parts, dst, cols):
        if offs % 8 == 0:
            for p in range(n):
                span = slice(p * offs, (p + 1) * offs)
                dst[p, :, cols] = jnp.concatenate([x[span] for x in parts], axis=0).astype(BF16)
        else:
            order = onehot(place((rows, rows), 0) == iota((rows, rows), 1))
            whole = jnp.concatenate(parts, axis=0).astype(BF16)
            dst[:, :, cols] = dot(order, whole).astype(BF16).reshape(n, chunk, tile)

    def from_chunks(src, cols):
        if offs % 8 == 0:
            pieces = [src[p, :, cols].astype(F32) for p in range(n)]
            return [
                jnp.concatenate([x[b * offs : (b + 1) * offs] for x in pieces], axis=0)
                for b in range(blocks)
            ]
        order = onehot(place((rows, rows), 1) == iota((rows, rows), 0))
        whole = dot(order, src[:, :, cols].reshape(rows, tile))
        return [whole[b * bs : (b + 1) * bs] for b in range(blocks)]

    @pl.loop(0, ndp - 1)
    def _(i):
        beside(0, w_ref, wg, mate(i), core).start()
        beside(1, mx_ref, mg, mate(i), core).start()

    def gate(cols):
        parts = []
        for b in range(blocks):
            span = slice(b * bs, (b + 1) * bs)
            parts.append(c_ref[span, cols].astype(F32) * q_ref[span, cols].astype(F32))
        to_chunks(parts, gs, cols)

    columns(gate)
    exchange(G, gs, gr)

    wg[core] = w_ref[...]
    mg[core] = mx_ref[...]

    @pl.loop(0, ndp - 1)
    def _(i):
        beside(0, w_ref, wg, core, mate(i)).wait_recv()
        beside(1, mx_ref, mg, core, mate(i)).wait_recv()

    for h in range(ndp):
        wfull[:, h * a_loc : (h + 1) * a_loc, :] = wg[h]

    def first(cols):
        parts = []
        for b in range(blocks):
            span = slice(b * bs, (b + 1) * bs)
            x = (k_ref[span, cols].astype(F32) * v_ref[span, cols].astype(F32)).astype(BF16)
            prod[span, cols] = x
            parts.append(dot(wfull[b], x))
        to_chunks(parts, fs, cols)

    columns(first)
    exchange(F, fs, fr)

    named = jnp.zeros((nb, nb), F32)
    index = bi_ref[...]
    for t in range(nnz):
        named = jnp.where(index[:, t : t + 1] == iota((nb, nb), 1), 1.0, named)
    named = named.astype(BF16)
    spread = onehot((iota((nb, rows), 1) >> log2(offs)) == iota((nb, rows), 0))
    same = ((iota((part, rows), 0) ^ iota((part, rows), 1)) & (offs - 1)) == 0
    r, c = iota((part, part), 0), iota((part, part), 1)
    by_block = onehot((r & (offs - 1)) * own + (r >> log2(offs)) == c)
    by_offset = onehot((c & (offs - 1)) * own + (c >> log2(offs)) == r)
    for h in range(ndp):
        span = slice(h * part, (h + 1) * part)
        lift = onehot((iota((part, nb), 0) >> log2(offs)) + h * own == iota((part, nb), 1))
        pattern = dot(lift, named)
        pr[h] = pattern
        masked = (dot(by_block, mg[h]) * pattern).astype(BF16)
        bmat[span, :] = jnp.where(same, dot(masked, spread), 0.0).astype(BF16)
    btm[...] = bmat[...].T

    def flat(ref, cols):
        return ref[:, :, cols].reshape(rows, tile)

    arrived(G, gs, gr)

    def grad_first(cols):
        hs[:, :, cols] = dot(btm[...], flat(gr, cols)).astype(BF16).reshape(n, chunk, tile)

    columns(grad_first)
    exchange(H, hs, hr)
    arrived(F, fs, fr)

    def mixed(cols):
        ms[:, :, cols] = dot(bmat[...], flat(fr, cols)).astype(BF16).reshape(n, chunk, tile)

    columns(mixed)
    exchange(M, ms, mr)

    step = part // chunk
    for h in range(ndp):
        lhs = gr[h * step : (h + 1) * step].reshape(part, width)
        terms = jnp.where(same, dot_nt(lhs, fr[...].reshape(rows, width)), 0.0)
        kept = sum(dot_nt(x, spread) for x in thirds(terms))
        gms[h] = kept * pr[h]

    @pl.loop(0, ndp - 1)
    def _(i):
        beside(2, gms.at[mate(i)], gmr, mate(i), core).start()

    arrived(H, hs, hr)

    def grad_inputs(cols):
        parts = from_chunks(hr, cols)
        for b in range(blocks):
            span = slice(b * bs, (b + 1) * bs)
            x = parts[b].astype(BF16)
            gfn[span, cols] = x
            gp = dot_tn(wfull[b], x)
            gk_ref[span, cols] = (gp * v_ref[span, cols].astype(F32)).astype(BF16)
            gv_ref[span, cols] = (gp * k_ref[span, cols].astype(F32)).astype(BF16)

    columns(grad_inputs)
    for b in range(blocks):
        span = slice(b * bs, (b + 1) * bs)
        terms = dot_nt(gfn[span, :], prod[span, :])
        for h in range(ndp):
            gbs[h, b] = terms[h * a_loc : (h + 1) * a_loc]

    @pl.loop(0, ndp - 1)
    def _(i):
        beside(3, gbs.at[mate(i)], gbr, mate(i), core).start()

    gmr[core] = gms[core]
    gbr[core] = gbs[core]

    @pl.loop(0, ndp - 1)
    def _(i):
        beside(2, gms.at[mate(i)], gmr, core, mate(i)).wait_recv()
        beside(3, gbs.at[mate(i)], gbr, core, mate(i)).wait_recv()

    gb_ref[...] = sum(gbr[h] for h in range(ndp))
    total = sum(gmr[h] for h in range(ndp))
    gm_ref[...] = sum(dot(by_offset, x) for x in thirds(total))

    @pl.loop(0, ndp - 1)
    def _(i):
        beside(0, w_ref, wg, mate(i), core).wait_send()
        beside(1, mx_ref, mg, mate(i), core).wait_send()
        beside(2, gms.at[mate(i)], gmr, mate(i), core).wait_send()
        beside(3, gbs.at[mate(i)], gbr, mate(i), core).wait_send()

    left(G, gs, gr)
    left(F, fs, fr)
    left(H, hs, hr)
    arrived(M, ms, mr)

    def outputs(cols):
        parts = from_chunks(mr, cols)
        for b in range(blocks):
            span = slice(b * bs, (b + 1) * bs)
            o_ref[span, cols] = (q_ref[span, cols].astype(F32) * parts[b]).astype(BF16)
            gq_ref[span, cols] = (c_ref[span, cols].astype(F32) * parts[b]).astype(BF16)

    columns(outputs)
    left(M, ms, mr)


def on_device(n, ndp, query, key, value, block_weights, mix_weights, block_index, cotangent):
    _, rows, width = query.shape
    nb = block_index.shape[0]
    blocks, a_loc, bs = block_weights.shape
    offs, own, _ = mix_weights.shape
    chunk, part = blocks * offs, own * offs
    wide = jax.ShapeDtypeStruct((rows, width), BF16)
    vmem = pl.BlockSpec(memory_space=pltpu.VMEM)
    moved = pltpu.VMEM((n, chunk, width), BF16)
    dma = pltpu.SemaphoreType.DMA
    outs = pl.pallas_call(
        functools.partial(kernel, n, ndp, 256),
        out_shape=(
            wide, wide, wide, wide,
            jax.ShapeDtypeStruct((blocks, a_loc, bs), F32),
            jax.ShapeDtypeStruct((offs * own, nb), F32),
        ),
        in_specs=[vmem] * 7,
        out_specs=(vmem,) * 6,
        scratch_shapes=[moved] * 8 + [
            pltpu.VMEM((rows, width), BF16),
            pltpu.VMEM((rows, width), BF16),
            pltpu.VMEM((rows, rows), BF16),
            pltpu.VMEM((rows, rows), BF16),
            pltpu.VMEM((blocks, bs, bs), BF16),
            pltpu.VMEM((ndp, blocks, a_loc, bs), BF16),
            pltpu.VMEM((ndp, offs * own, nb), BF16),
            pltpu.VMEM((ndp, part, nb), F32),
            pltpu.VMEM((ndp, part, nb), F32),
            pltpu.VMEM((ndp, part, nb), F32),
            pltpu.VMEM((ndp, blocks, a_loc, bs), F32),
            pltpu.VMEM((ndp, blocks, a_loc, bs), F32),
            dma((4, n)), dma((4, n)), dma((4, ndp)), dma((4, ndp)), dma((4,)), dma((8,)),
        ],
        compiler_params=pltpu.CompilerParams(
            collective_id=0, has_side_effects=True, vmem_limit_bytes=56 * 1024 * 1024
        ),
        cost_estimate=pl.CostEstimate(
            flops=7 * 2 * rows * rows * width, bytes_accessed=16 * rows * width, transcendentals=0
        ),
        name="monarch",
    )(
        query[0], key[0], value[0], cotangent[0],
        block_weights, mix_weights.reshape(offs * own, nb), block_index,
    )
    output, grad_query, grad_key, grad_value, grad_blocks, grad_mix = outs
    return (
        output[None], grad_query[None], grad_key[None], grad_value[None],
        grad_blocks, grad_mix.reshape(offs, own, nb),
    )


def solution(mesh):
    wide, split = P("dp", "seq", None), P("seq", "dp", None)
    return jax.shard_map(
        functools.partial(on_device, mesh.shape["seq"], mesh.shape["dp"]),
        mesh=mesh,
        in_specs=(wide, wide, wide, split, split, P(), wide),
        out_specs=(wide, wide, wide, wide, split, split),
        check_vma=False,
    )
```

```python
import functools

import jax
import jax.numpy as jnp
from jax import lax
from jax.experimental import pallas as pl
from jax.experimental.pallas import tpu as pltpu
from jax.sharding import PartitionSpec as P

F32 = jnp.float32
BF16 = jnp.bfloat16
G, F, H, M = range(4)


def log2(x):
    return x.bit_length() - 1


def iota(shape, dim):
    return lax.broadcasted_iota(jnp.int32, shape, dim)


def onehot(cond):
    return jnp.where(cond, 1.0, 0.0).astype(BF16)


def dot(a, b):
    return jnp.dot(a, b, preferred_element_type=F32)


def dot_nt(a, b):
    return lax.dot_general(a, b, (((1,), (1,)), ((), ())), preferred_element_type=F32)


def dot_tn(a, b):
    return lax.dot_general(a, b, (((0,), (0,)), ((), ())), preferred_element_type=F32)


def thirds(x):
    hi = x.astype(BF16)
    rest = x - hi.astype(F32)
    mid = rest.astype(BF16)
    return hi, mid, (rest - mid.astype(F32)).astype(BF16)


def kernel(
    n, ndp, halves, tile,
    q_in, k_in, v_in, c_in, w_ref, mx_ref, bi_ref,
    o_ref, gq_ref, gk_ref, gv_ref, gb_ref, gm_ref,
    gs, gr, fs, fr, hs, hr, ms, mr,
    prod, gfn, bmat, btm, wfull, wg, mg, pr, gms, gmr, gbs, gbr,
    q_ref, k_ref, v_ref, c_ref,
    send, recv, dsend, drecv, lsem, isem,
):
    rows, width = q_ref.shape
    blocks, bs = w_ref.shape[0], w_ref.shape[2]
    nnz, nb = bi_ref.shape
    offs = bs // n
    chunk = blocks * offs
    own = nb // ndp
    part = own * offs
    a_loc = w_ref.shape[1]
    me = lax.axis_index("seq")
    core = lax.axis_index("dp")

    def peer(i):
        return lax.rem(me + 1 + lax.rem(n // 2 - 1 + 4 * i, n - 1), n)

    def mate(i):
        return lax.rem(core + 1 + i, ndp)

    half = width // halves

    def fetch(u, kind):
        src = (c_in, q_in, k_in, v_in)[kind]
        dst = (c_ref, q_ref, k_ref, v_ref)[kind]
        span = slice(u * half, (u + 1) * half)
        return pltpu.make_async_copy(src.at[:, span], dst.at[:, span], isem.at[u, kind])

    for kinds in ((0, 1), (2, 3)):
        for u in range(halves):
            for kind in kinds:
                fetch(u, kind).start()

    barrier = pltpu.get_barrier_semaphore()

    @pl.loop(0, n - 1)
    def _(i):
        pl.semaphore_signal(
            barrier, inc=1, device_id={"dp": core, "seq": lax.rem(me + 1 + i, n)},
            device_id_type=pl.DeviceIdType.MESH,
        )

    @pl.loop(0, ndp - 1)
    def _(i):
        pl.semaphore_signal(
            barrier, inc=1, device_id={"dp": mate(i), "seq": me},
            device_id_type=pl.DeviceIdType.MESH,
        )

    pl.semaphore_wait(barrier, n + ndp - 2)

    def across(kind, u, src, dst, to, slot):
        return pltpu.make_async_remote_copy(
            src_ref=src.at[u, to], dst_ref=dst.at[u, slot],
            send_sem=send.at[kind, u, to], recv_sem=recv.at[kind, u, slot],
            device_id={"dp": core, "seq": to}, device_id_type=pl.DeviceIdType.MESH,
        )

    pairs = ((gs, gr), (fs, fr), (hs, hr), (ms, mr))

    def exchange(kind, u):
        src, dst = pairs[kind]
        before = kind * halves + u - 2

        @pl.loop(0, n - 1)
        def _(i):
            if before >= 0:
                across(before // halves, before % halves, *pairs[before // halves], peer(i), me).wait_send()
            across(kind, u, src, dst, peer(i), me).start()

        pltpu.make_async_copy(src.at[u, me], dst.at[u, me], lsem.at[kind, u]).start()

    def arrived(kind, u):
        src, dst = pairs[kind]

        @pl.loop(0, n - 1)
        def _(i):
            across(kind, u, src, dst, me, peer(i)).wait_recv()

        pltpu.make_async_copy(src.at[u, me], dst.at[u, me], lsem.at[kind, u]).wait()

    def left(kind, u):
        @pl.loop(0, n - 1)
        def _(i):
            across(kind, u, *pairs[kind], peer(i), me).wait_send()

    def beside(kind, src, dst, to, slot):
        return pltpu.make_async_remote_copy(
            src_ref=src, dst_ref=dst.at[slot],
            send_sem=dsend.at[kind, to], recv_sem=drecv.at[kind, slot],
            device_id={"dp": to, "seq": me}, device_id_type=pl.DeviceIdType.MESH,
        )

    def columns(u, body):
        @pl.loop(0, half // tile)
        def _(t):
            start = pl.multiple_of(t * tile, tile)
            body(pl.ds(u * half + start, tile), pl.ds(start, tile))

    def place(shape, row_dim):
        r = iota(shape, row_dim)
        rem = r & (chunk - 1)
        return (rem >> log2(offs)) * bs + (r >> log2(chunk)) * offs + (rem & (offs - 1))

    def to_chunks(parts, dst, u, cols):
        if offs % 8 == 0:
            for p in range(n):
                span = slice(p * offs, (p + 1) * offs)
                dst[u, p, :, cols] = jnp.concatenate([x[span] for x in parts], axis=0).astype(BF16)
        else:
            order = onehot(place((rows, rows), 0) == iota((rows, rows), 1))
            whole = jnp.concatenate(parts, axis=0).astype(BF16)
            dst[u, :, :, cols] = dot(order, whole).astype(BF16).reshape(n, chunk, tile)

    def from_chunks(src, u, cols):
        if offs % 8 == 0:
            pieces = [src[u, p, :, cols].astype(F32) for p in range(n)]
            return [
                jnp.concatenate([x[b * offs : (b + 1) * offs] for x in pieces], axis=0)
                for b in range(blocks)
            ]
        order = onehot(place((rows, rows), 1) == iota((rows, rows), 0))
        whole = dot(order, src[u, :, :, cols].reshape(rows, tile))
        return [whole[b * bs : (b + 1) * bs] for b in range(blocks)]

    @pl.loop(0, ndp - 1)
    def _(i):
        beside(0, w_ref, wg, mate(i), core).start()
        beside(1, mx_ref, mg, mate(i), core).start()

    for u in range(halves):
        fetch(u, 0).wait()
        fetch(u, 1).wait()

        def gate(cols, at):
            parts = []
            for b in range(blocks):
                span = slice(b * bs, (b + 1) * bs)
                parts.append(c_ref[span, cols].astype(F32) * q_ref[span, cols].astype(F32))
            to_chunks(parts, gs, u, at)

        columns(u, gate)
        exchange(G, u)

    wg[core] = w_ref[...]
    mg[core] = mx_ref[...]

    @pl.loop(0, ndp - 1)
    def _(i):
        beside(0, w_ref, wg, core, mate(i)).wait_recv()
        beside(1, mx_ref, mg, core, mate(i)).wait_recv()

    for h in range(ndp):
        wfull[:, h * a_loc : (h + 1) * a_loc, :] = wg[h]

    for u in range(halves):
        fetch(u, 2).wait()
        fetch(u, 3).wait()

        def first(cols, at):
            parts = []
            for b in range(blocks):
                span = slice(b * bs, (b + 1) * bs)
                x = (k_ref[span, cols].astype(F32) * v_ref[span, cols].astype(F32)).astype(BF16)
                prod[span, cols] = x
                parts.append(dot(wfull[b], x))
            to_chunks(parts, fs, u, at)

        columns(u, first)

    named = jnp.zeros((nb, nb), F32)
    index = bi_ref[...]
    for t in range(nnz):
        named = jnp.where(index[t : t + 1, :] == iota((nb, nb), 0), 1.0, named)
    named = named.astype(BF16)
    spread = onehot((iota((nb, rows), 1) >> log2(offs)) == iota((nb, rows), 0))
    same = ((iota((part, rows), 0) ^ iota((part, rows), 1)) & (offs - 1)) == 0
    r, c = iota((part, part), 0), iota((part, part), 1)
    by_block = onehot((r & (offs - 1)) * own + (r >> log2(offs)) == c)
    by_offset = onehot((c & (offs - 1)) * own + (c >> log2(offs)) == r)
    for h in range(ndp):
        span = slice(h * part, (h + 1) * part)
        lift = onehot((iota((part, nb), 0) >> log2(offs)) + h * own == iota((part, nb), 1))
        pattern = dot_nt(lift, named)
        pr[h] = pattern
        masked = (dot(by_block, mg[h]) * pattern).astype(BF16)
        bmat[span, :] = jnp.where(same, dot(masked, spread), 0.0).astype(BF16)
    btm[...] = bmat[...].T

    for u in range(halves):
        exchange(F, u)

    def second(matrix, kind, u, back):
        src, dst = pairs[kind][1], pairs[back][0]
        arrived(kind, u)

        def body(cols, at):
            x = src[u, :, :, at].reshape(rows, tile)
            dst[u, :, :, at] = dot(matrix[...], x).astype(BF16).reshape(n, chunk, tile)

        columns(u, body)
        exchange(back, u)

    for u in range(halves):
        second(btm, G, u, H)
    for u in range(halves):
        second(bmat, F, u, M)

    step = part // chunk
    for h in range(ndp):
        span = slice(h * step, (h + 1) * step)
        terms = sum(
            dot_nt(gr[u, span].reshape(part, half), fr[u].reshape(rows, half))
            for u in range(halves)
        )
        terms = jnp.where(same, terms, 0.0)
        kept = sum(dot_nt(x, spread) for x in thirds(terms))
        gms[h] = kept * pr[h]

    @pl.loop(0, ndp - 1)
    def _(i):
        beside(2, gms.at[mate(i)], gmr, mate(i), core).start()

    for u in range(halves):
        arrived(H, u)

        def grad_inputs(cols, at):
            parts = from_chunks(hr, u, at)
            for b in range(blocks):
                span = slice(b * bs, (b + 1) * bs)
                x = parts[b].astype(BF16)
                gfn[span, cols] = x
                gp = dot_tn(wfull[b], x)
                gk_ref[span, cols] = (gp * v_ref[span, cols].astype(F32)).astype(BF16)
                gv_ref[span, cols] = (gp * k_ref[span, cols].astype(F32)).astype(BF16)

        columns(u, grad_inputs)

    for b in range(blocks):
        span = slice(b * bs, (b + 1) * bs)
        terms = dot_nt(gfn[span, :], prod[span, :])
        for h in range(ndp):
            gbs[h, b] = terms[h * a_loc : (h + 1) * a_loc]

    @pl.loop(0, ndp - 1)
    def _(i):
        beside(3, gbs.at[mate(i)], gbr, mate(i), core).start()

    gmr[core] = gms[core]
    gbr[core] = gbs[core]

    @pl.loop(0, ndp - 1)
    def _(i):
        beside(2, gms.at[mate(i)], gmr, core, mate(i)).wait_recv()
        beside(3, gbs.at[mate(i)], gbr, core, mate(i)).wait_recv()

    gb_ref[...] = sum(gbr[h] for h in range(ndp))
    total = sum(gmr[h] for h in range(ndp))
    gm_ref[...] = sum(dot(by_offset, x) for x in thirds(total))

    @pl.loop(0, ndp - 1)
    def _(i):
        beside(0, w_ref, wg, mate(i), core).wait_send()
        beside(1, mx_ref, mg, mate(i), core).wait_send()
        beside(2, gms.at[mate(i)], gmr, mate(i), core).wait_send()
        beside(3, gbs.at[mate(i)], gbr, mate(i), core).wait_send()

    for u in range(halves):
        arrived(M, u)

        def outputs(cols, at):
            parts = from_chunks(mr, u, at)
            for b in range(blocks):
                span = slice(b * bs, (b + 1) * bs)
                o_ref[span, cols] = (q_ref[span, cols].astype(F32) * parts[b]).astype(BF16)
                gq_ref[span, cols] = (c_ref[span, cols].astype(F32) * parts[b]).astype(BF16)

        columns(u, outputs)

    for last in range(4 * halves - 2, 4 * halves):
        left(last // halves, last % halves)


def write_out(*refs):
    count = len(refs) // 2
    sems = refs[-1]
    copies = [
        pltpu.make_async_copy(refs[i], refs[count + i], sems.at[i]) for i in range(count)
    ]
    for copy in copies:
        copy.start()
    for copy in copies:
        copy.wait()


def on_device(n, ndp, query, key, value, block_weights, mix_weights, block_index, cotangent):
    _, rows, width = query.shape
    nb = block_index.shape[0]
    blocks, a_loc, bs = block_weights.shape
    offs, own, _ = mix_weights.shape
    chunk, part = blocks * offs, own * offs
    vmem = pl.BlockSpec(memory_space=pltpu.VMEM)
    anywhere = pl.BlockSpec(memory_space=pl.ANY)
    halves = 2
    moved = pltpu.VMEM((halves, n, chunk, width // halves), BF16)
    shapes = [((rows, width), BF16)] * 4 + [((blocks, a_loc, bs), F32), ((offs * own, nb), F32)]
    dma = pltpu.SemaphoreType.DMA
    outs = pl.pallas_call(
        functools.partial(kernel, n, ndp, halves, 256),
        out_shape=tuple(pltpu.VMEM(*shape) for shape in shapes),
        in_specs=[anywhere] * 4 + [vmem] * 3,
        out_specs=(vmem,) * 6,
        scratch_shapes=[moved] * 8 + [
            pltpu.VMEM((rows, width), BF16),
            pltpu.VMEM((rows, width), BF16),
            pltpu.VMEM((rows, rows), BF16),
            pltpu.VMEM((rows, rows), BF16),
            pltpu.VMEM((blocks, bs, bs), BF16),
            pltpu.VMEM((ndp, blocks, a_loc, bs), BF16),
            pltpu.VMEM((ndp, offs * own, nb), BF16),
            pltpu.VMEM((ndp, part, nb), F32),
            pltpu.VMEM((ndp, part, nb), F32),
            pltpu.VMEM((ndp, part, nb), F32),
            pltpu.VMEM((ndp, blocks, a_loc, bs), F32),
            pltpu.VMEM((ndp, blocks, a_loc, bs), F32),
            *[pltpu.VMEM((rows, width), BF16)] * 4,
            dma((4, halves, n)), dma((4, halves, n)), dma((4, ndp)), dma((4, ndp)),
            dma((4, halves)), dma((halves, 4)),
        ],
        compiler_params=pltpu.CompilerParams(
            collective_id=0, has_side_effects=True, vmem_limit_bytes=48 * 1024 * 1024
        ),
        cost_estimate=pl.CostEstimate(
            flops=7 * 2 * rows * rows * width, bytes_accessed=16 * rows * width, transcendentals=0
        ),
        name="monarch",
    )(
        query[0], key[0], value[0], cotangent[0],
        block_weights, mix_weights.reshape(offs * own, nb), block_index.T,
    )
    outs = pl.pallas_call(
        write_out,
        out_shape=tuple(jax.ShapeDtypeStruct(*shape) for shape in shapes),
        in_specs=[vmem] * 6,
        out_specs=(anywhere,) * 6,
        scratch_shapes=[dma((6,))],
        name="write_out",
    )(*outs)
    output, grad_query, grad_key, grad_value, grad_blocks, grad_mix = outs
    return (
        output[None], grad_query[None], grad_key[None], grad_value[None],
        grad_blocks, grad_mix.reshape(offs, own, nb),
    )


def solution(mesh):
    wide, split = P("dp", "seq", None), P("seq", "dp", None)
    return jax.shard_map(
        functools.partial(on_device, mesh.shape["seq"], mesh.shape["dp"]),
        mesh=mesh,
        in_specs=(wide, wide, wide, split, split, P(), wide),
        out_specs=(wide, wide, wide, wide, split, split),
        check_vma=False,
    )
```

```python
import functools

import jax
import jax.numpy as jnp
from jax import lax
from jax.experimental import pallas as pl
from jax.experimental.pallas import tpu as pltpu
from jax.sharding import PartitionSpec as P

F32 = jnp.float32
BF16 = jnp.bfloat16
G, F, H, M = range(4)


def log2(x):
    return x.bit_length() - 1


def iota(shape, dim):
    return lax.broadcasted_iota(jnp.int32, shape, dim)


def onehot(cond):
    return jnp.where(cond, 1.0, 0.0).astype(BF16)


def dot(a, b):
    return jnp.dot(a, b, preferred_element_type=F32)


def dot_nt(a, b):
    return lax.dot_general(a, b, (((1,), (1,)), ((), ())), preferred_element_type=F32)


def dot_tn(a, b):
    return lax.dot_general(a, b, (((0,), (0,)), ((), ())), preferred_element_type=F32)


def thirds(x):
    hi = x.astype(BF16)
    rest = x - hi.astype(F32)
    mid = rest.astype(BF16)
    return hi, mid, (rest - mid.astype(F32)).astype(BF16)


def kernel(
    n, ndp, cuts, tile,
    q_in, k_in, v_in, c_in, w_ref, mx_ref, bi_ref,
    o_ref, gq_ref, gk_ref, gv_ref, gb_ref, gm_ref,
    gs, gr, fs, fr, hs, hr, ms, mr,
    prod, gfn, bmat, btm, wfull, wg, mg, pr, gms, gmr, gbs, gbr,
    q_ref, k_ref, v_ref, c_ref,
    send, recv, dsend, drecv, lsem, isem,
):
    rows, width = q_ref.shape
    blocks, bs = w_ref.shape[0], w_ref.shape[2]
    nnz, nb = bi_ref.shape
    offs = bs // n
    chunk = blocks * offs
    own = nb // ndp
    part = own * offs
    a_loc = w_ref.shape[1]
    me = lax.axis_index("seq")
    core = lax.axis_index("dp")

    def peer(i):
        return lax.rem(me + 1 + lax.rem(n // 2 - 1 + 4 * i, n - 1), n)

    def mate(i):
        return lax.rem(core + 1 + i, ndp)

    piece = width // cuts
    depth = cuts

    def fetch(u, kind):
        src = (c_in, q_in, k_in, v_in)[kind]
        dst = (c_ref, q_ref, k_ref, v_ref)[kind]
        span = slice(u * piece, (u + 1) * piece)
        return pltpu.make_async_copy(src.at[:, span], dst.at[:, span], isem.at[u, kind])

    for kinds in ((0, 1), (2, 3)):
        for u in range(cuts):
            for kind in kinds:
                fetch(u, kind).start()

    barrier = pltpu.get_barrier_semaphore()

    @pl.loop(0, n - 1)
    def _(i):
        pl.semaphore_signal(
            barrier, inc=1, device_id={"dp": core, "seq": lax.rem(me + 1 + i, n)},
            device_id_type=pl.DeviceIdType.MESH,
        )

    @pl.loop(0, ndp - 1)
    def _(i):
        pl.semaphore_signal(
            barrier, inc=1, device_id={"dp": mate(i), "seq": me},
            device_id_type=pl.DeviceIdType.MESH,
        )

    def across(kind, u, src, dst, to, slot):
        return pltpu.make_async_remote_copy(
            src_ref=src.at[u, to], dst_ref=dst.at[u, slot],
            send_sem=send.at[kind, u, to], recv_sem=recv.at[kind, u, slot],
            device_id={"dp": core, "seq": to}, device_id_type=pl.DeviceIdType.MESH,
        )

    pairs = ((gs, gr), (fs, fr), (hs, hr), (ms, mr))

    def exchange(kind, u):
        src, dst = pairs[kind]
        before = kind * cuts + u - depth

        @pl.loop(0, n - 1)
        def _(i):
            if before >= 0:
                across(before // cuts, before % cuts, *pairs[before // cuts], peer(i), me).wait_send()
            across(kind, u, src, dst, peer(i), me).start()

        pltpu.make_async_copy(src.at[u, me], dst.at[u, me], lsem.at[kind, u]).start()

    def arrived(kind, u):
        src, dst = pairs[kind]

        @pl.loop(0, n - 1)
        def _(i):
            across(kind, u, src, dst, me, peer(i)).wait_recv()

        pltpu.make_async_copy(src.at[u, me], dst.at[u, me], lsem.at[kind, u]).wait()

    def left(kind, u):
        @pl.loop(0, n - 1)
        def _(i):
            across(kind, u, *pairs[kind], peer(i), me).wait_send()

    def beside(kind, src, dst, to, slot):
        return pltpu.make_async_remote_copy(
            src_ref=src, dst_ref=dst.at[slot],
            send_sem=dsend.at[kind, to], recv_sem=drecv.at[kind, slot],
            device_id={"dp": to, "seq": me}, device_id_type=pl.DeviceIdType.MESH,
        )

    def columns(u, body):
        @pl.loop(0, piece // tile)
        def _(t):
            start = pl.multiple_of(t * tile, tile)
            body(pl.ds(u * piece + start, tile), pl.ds(start, tile))

    def place(shape, row_dim):
        r = iota(shape, row_dim)
        rem = r & (chunk - 1)
        return (rem >> log2(offs)) * bs + (r >> log2(chunk)) * offs + (rem & (offs - 1))

    def to_chunks(parts, dst, u, cols):
        if offs % 8 == 0:
            for p in range(n):
                span = slice(p * offs, (p + 1) * offs)
                dst[u, p, :, cols] = jnp.concatenate([x[span] for x in parts], axis=0).astype(BF16)
        else:
            order = onehot(place((rows, rows), 0) == iota((rows, rows), 1))
            whole = jnp.concatenate(parts, axis=0).astype(BF16)
            dst[u, :, :, cols] = dot(order, whole).astype(BF16).reshape(n, chunk, tile)

    def from_chunks(src, u, cols):
        if offs % 8 == 0:
            pieces = [src[u, p, :, cols].astype(F32) for p in range(n)]
            return [
                jnp.concatenate([x[b * offs : (b + 1) * offs] for x in pieces], axis=0)
                for b in range(blocks)
            ]
        order = onehot(place((rows, rows), 1) == iota((rows, rows), 0))
        whole = dot(order, src[u, :, :, cols].reshape(rows, tile))
        return [whole[b * bs : (b + 1) * bs] for b in range(blocks)]

    for u in range(cuts):
        fetch(u, 0).wait()
        fetch(u, 1).wait()

        def gate(cols, at):
            parts = []
            for b in range(blocks):
                span = slice(b * bs, (b + 1) * bs)
                parts.append(c_ref[span, cols].astype(F32) * q_ref[span, cols].astype(F32))
            to_chunks(parts, gs, u, at)

        columns(u, gate)
        if u == 0:
            pl.semaphore_wait(barrier, n + ndp - 2)
        exchange(G, u)

    @pl.loop(0, ndp - 1)
    def _(i):
        beside(0, w_ref, wg, mate(i), core).start()
        beside(1, mx_ref, mg, mate(i), core).start()

    wg[core] = w_ref[...]
    mg[core] = mx_ref[...]

    @pl.loop(0, ndp - 1)
    def _(i):
        beside(0, w_ref, wg, core, mate(i)).wait_recv()
        beside(1, mx_ref, mg, core, mate(i)).wait_recv()

    for h in range(ndp):
        wfull[:, h * a_loc : (h + 1) * a_loc, :] = wg[h]

    for u in range(cuts):
        fetch(u, 2).wait()
        fetch(u, 3).wait()

        def first(cols, at):
            parts = []
            for b in range(blocks):
                span = slice(b * bs, (b + 1) * bs)
                x = (k_ref[span, cols].astype(F32) * v_ref[span, cols].astype(F32)).astype(BF16)
                prod[span, cols] = x
                parts.append(dot(wfull[b], x))
            to_chunks(parts, fs, u, at)

        columns(u, first)

    named = jnp.zeros((nb, nb), F32)
    index = bi_ref[...]
    for t in range(nnz):
        named = jnp.where(index[t : t + 1, :] == iota((nb, nb), 0), 1.0, named)
    named = named.astype(BF16)
    spread = onehot((iota((nb, rows), 1) >> log2(offs)) == iota((nb, rows), 0))
    same = ((iota((part, rows), 0) ^ iota((part, rows), 1)) & (offs - 1)) == 0
    r, c = iota((part, part), 0), iota((part, part), 1)
    by_block = onehot((r & (offs - 1)) * own + (r >> log2(offs)) == c)
    by_offset = onehot((c & (offs - 1)) * own + (c >> log2(offs)) == r)
    for h in range(ndp):
        span = slice(h * part, (h + 1) * part)
        lift = onehot((iota((part, nb), 0) >> log2(offs)) + h * own == iota((part, nb), 1))
        pattern = dot_nt(lift, named)
        pr[h] = pattern
        masked = (dot(by_block, mg[h]) * pattern).astype(BF16)
        bmat[span, :] = jnp.where(same, dot(masked, spread), 0.0).astype(BF16)
    btm[...] = bmat[...].T

    for u in range(cuts):
        exchange(F, u)

    def second(matrix, kind, u, back):
        src, dst = pairs[kind][1], pairs[back][0]
        arrived(kind, u)

        def body(cols, at):
            x = src[u, :, :, at].reshape(rows, tile)
            dst[u, :, :, at] = dot(matrix[...], x).astype(BF16).reshape(n, chunk, tile)

        columns(u, body)
        exchange(back, u)

    for u in range(cuts):
        second(btm, G, u, H)
    for u in range(cuts):
        second(bmat, F, u, M)

    step = part // chunk
    for h in range(ndp):
        span = slice(h * step, (h + 1) * step)
        terms = sum(
            dot_nt(gr[u, span].reshape(part, piece), fr[u].reshape(rows, piece))
            for u in range(cuts)
        )
        terms = jnp.where(same, terms, 0.0)
        kept = sum(dot_nt(x, spread) for x in thirds(terms))
        gms[h] = kept * pr[h]

    @pl.loop(0, ndp - 1)
    def _(i):
        beside(2, gms.at[mate(i)], gmr, mate(i), core).start()

    for u in range(cuts):
        arrived(H, u)

        def grad_inputs(cols, at):
            parts = from_chunks(hr, u, at)
            for b in range(blocks):
                span = slice(b * bs, (b + 1) * bs)
                x = parts[b].astype(BF16)
                gfn[span, cols] = x
                gp = dot_tn(wfull[b], x)
                gk_ref[span, cols] = (gp * v_ref[span, cols].astype(F32)).astype(BF16)
                gv_ref[span, cols] = (gp * k_ref[span, cols].astype(F32)).astype(BF16)

        columns(u, grad_inputs)

    for b in range(blocks):
        span = slice(b * bs, (b + 1) * bs)
        terms = dot_nt(gfn[span, :], prod[span, :])
        for h in range(ndp):
            gbs[h, b] = terms[h * a_loc : (h + 1) * a_loc]

    @pl.loop(0, ndp - 1)
    def _(i):
        beside(3, gbs.at[mate(i)], gbr, mate(i), core).start()

    gmr[core] = gms[core]
    gbr[core] = gbs[core]

    @pl.loop(0, ndp - 1)
    def _(i):
        beside(2, gms.at[mate(i)], gmr, core, mate(i)).wait_recv()
        beside(3, gbs.at[mate(i)], gbr, core, mate(i)).wait_recv()

    gb_ref[...] = sum(gbr[h] for h in range(ndp))
    total = sum(gmr[h] for h in range(ndp))
    gm_ref[...] = sum(dot(by_offset, x) for x in thirds(total))

    @pl.loop(0, ndp - 1)
    def _(i):
        beside(0, w_ref, wg, mate(i), core).wait_send()
        beside(1, mx_ref, mg, mate(i), core).wait_send()
        beside(2, gms.at[mate(i)], gmr, mate(i), core).wait_send()
        beside(3, gbs.at[mate(i)], gbr, mate(i), core).wait_send()

    for u in range(cuts):
        arrived(M, u)

        def outputs(cols, at):
            parts = from_chunks(mr, u, at)
            for b in range(blocks):
                span = slice(b * bs, (b + 1) * bs)
                o_ref[span, cols] = (q_ref[span, cols].astype(F32) * parts[b]).astype(BF16)
                gq_ref[span, cols] = (c_ref[span, cols].astype(F32) * parts[b]).astype(BF16)

        columns(u, outputs)

    for last in range(4 * cuts - depth, 4 * cuts):
        left(last // cuts, last % cuts)


def write_out(*refs):
    count = len(refs) // 2
    sems = refs[-1]
    copies = [
        pltpu.make_async_copy(refs[i], refs[count + i], sems.at[i]) for i in range(count)
    ]
    for copy in copies:
        copy.start()
    for copy in copies:
        copy.wait()


def on_device(n, ndp, query, key, value, block_weights, mix_weights, block_index, cotangent):
    _, rows, width = query.shape
    nb = block_index.shape[0]
    blocks, a_loc, bs = block_weights.shape
    offs, own, _ = mix_weights.shape
    chunk, part = blocks * offs, own * offs
    vmem = pl.BlockSpec(memory_space=pltpu.VMEM)
    anywhere = pl.BlockSpec(memory_space=pl.ANY)
    cuts = 3
    moved = pltpu.VMEM((cuts, n, chunk, width // cuts), BF16)
    shapes = [((rows, width), BF16)] * 4 + [((blocks, a_loc, bs), F32), ((offs * own, nb), F32)]
    dma = pltpu.SemaphoreType.DMA
    outs = pl.pallas_call(
        functools.partial(kernel, n, ndp, cuts, 256),
        out_shape=tuple(pltpu.VMEM(*shape) for shape in shapes),
        in_specs=[anywhere] * 4 + [vmem] * 3,
        out_specs=(vmem,) * 6,
        scratch_shapes=[moved] * 8 + [
            pltpu.VMEM((rows, width), BF16),
            pltpu.VMEM((rows, width), BF16),
            pltpu.VMEM((rows, rows), BF16),
            pltpu.VMEM((rows, rows), BF16),
            pltpu.VMEM((blocks, bs, bs), BF16),
            pltpu.VMEM((ndp, blocks, a_loc, bs), BF16),
            pltpu.VMEM((ndp, offs * own, nb), BF16),
            pltpu.VMEM((ndp, part, nb), F32),
            pltpu.VMEM((ndp, part, nb), F32),
            pltpu.VMEM((ndp, part, nb), F32),
            pltpu.VMEM((ndp, blocks, a_loc, bs), F32),
            pltpu.VMEM((ndp, blocks, a_loc, bs), F32),
            *[pltpu.VMEM((rows, width), BF16)] * 4,
            dma((4, cuts, n)), dma((4, cuts, n)), dma((4, ndp)), dma((4, ndp)),
            dma((4, cuts)), dma((cuts, 4)),
        ],
        compiler_params=pltpu.CompilerParams(
            collective_id=0, has_side_effects=True, vmem_limit_bytes=48 * 1024 * 1024
        ),
        cost_estimate=pl.CostEstimate(
            flops=7 * 2 * rows * rows * width, bytes_accessed=16 * rows * width, transcendentals=0
        ),
        name="monarch",
    )(
        query[0], key[0], value[0], cotangent[0],
        block_weights, mix_weights.reshape(offs * own, nb), block_index.T,
    )
    outs = pl.pallas_call(
        write_out,
        out_shape=tuple(jax.ShapeDtypeStruct(*shape) for shape in shapes),
        in_specs=[vmem] * 6,
        out_specs=(anywhere,) * 6,
        scratch_shapes=[dma((6,))],
        compiler_params=pltpu.CompilerParams(vmem_limit_bytes=8 * 1024 * 1024),
        name="write_out",
    )(*outs)
    output, grad_query, grad_key, grad_value, grad_blocks, grad_mix = outs
    return (
        output[None], grad_query[None], grad_key[None], grad_value[None],
        grad_blocks, grad_mix.reshape(offs, own, nb),
    )


def solution(mesh):
    wide, split = P("dp", "seq", None), P("seq", "dp", None)
    return jax.shard_map(
        functools.partial(on_device, mesh.shape["seq"], mesh.shape["dp"]),
        mesh=mesh,
        in_specs=(wide, wide, wide, split, split, P(), wide),
        out_specs=(wide, wide, wide, wide, split, split),
        check_vma=False,
    )
```

```python
import functools

import jax
import jax.numpy as jnp
from jax import lax
from jax.experimental import pallas as pl
from jax.experimental.pallas import tpu as pltpu
from jax.sharding import PartitionSpec as P

F32 = jnp.float32
BF16 = jnp.bfloat16
G, F, H, M = range(4)


def log2(x):
    return x.bit_length() - 1


def iota(shape, dim):
    return lax.broadcasted_iota(jnp.int32, shape, dim)


def onehot(cond):
    return jnp.where(cond, 1.0, 0.0).astype(BF16)


def dot(a, b):
    return jnp.dot(a, b, preferred_element_type=F32)


def dot_nt(a, b):
    return lax.dot_general(a, b, (((1,), (1,)), ((), ())), preferred_element_type=F32)


def dot_tn(a, b):
    return lax.dot_general(a, b, (((0,), (0,)), ((), ())), preferred_element_type=F32)


def thirds(x):
    hi = x.astype(BF16)
    rest = x - hi.astype(F32)
    mid = rest.astype(BF16)
    return hi, mid, (rest - mid.astype(F32)).astype(BF16)


def kernel(
    n, ndp, cuts, tile,
    q_in, k_in, v_in, c_in, w_ref, mx_ref, bi_ref,
    o_ref, gq_ref, gk_ref, gv_ref, gb_ref, gm_ref,
    gs, gr, fs, fr, hs, hr, ms, mr,
    prod, gfn, bmat, btm, wfull, wg, mg, pr, gms, gmr, gbs, gbr,
    q_ref, k_ref, v_ref, c_ref,
    send, recv, dsend, drecv, lsem, isem,
):
    rows, width = q_ref.shape
    blocks, bs = w_ref.shape[0], w_ref.shape[2]
    nnz, nb = bi_ref.shape
    offs = bs // n
    chunk = blocks * offs
    own = nb // ndp
    part = own * offs
    a_loc = w_ref.shape[1]
    me = lax.axis_index("seq")
    core = lax.axis_index("dp")

    def peer(i):
        return lax.rem(me + 1 + lax.rem(n // 2 - 1 + 4 * (i + 2 * core), n - 1), n)

    def mate(i):
        return lax.rem(core + 1 + i, ndp)

    piece = width // cuts
    depth = cuts

    def fetch(u, kind):
        src = (c_in, q_in, k_in, v_in)[kind]
        dst = (c_ref, q_ref, k_ref, v_ref)[kind]
        span = slice(u * piece, (u + 1) * piece)
        return pltpu.make_async_copy(src.at[:, span], dst.at[:, span], isem.at[u, kind])

    for kinds in ((0, 1), (2, 3)):
        for u in range(cuts):
            for kind in kinds:
                fetch(u, kind).start()

    barrier = pltpu.get_barrier_semaphore()

    @pl.loop(0, n - 1)
    def _(i):
        pl.semaphore_signal(
            barrier, inc=1, device_id={"dp": core, "seq": lax.rem(me + 1 + i, n)},
            device_id_type=pl.DeviceIdType.MESH,
        )

    @pl.loop(0, ndp - 1)
    def _(i):
        pl.semaphore_signal(
            barrier, inc=1, device_id={"dp": mate(i), "seq": me},
            device_id_type=pl.DeviceIdType.MESH,
        )

    def across(kind, u, src, dst, to, slot):
        return pltpu.make_async_remote_copy(
            src_ref=src.at[u, to], dst_ref=dst.at[u, slot],
            send_sem=send.at[kind, u, to], recv_sem=recv.at[kind, u, slot],
            device_id={"dp": core, "seq": to}, device_id_type=pl.DeviceIdType.MESH,
        )

    pairs = ((gs, gr), (fs, fr), (hs, hr), (ms, mr))

    def exchange(kind, u):
        src, dst = pairs[kind]
        before = kind * cuts + u - depth

        @pl.loop(0, n - 1)
        def _(i):
            if before >= 0:
                across(before // cuts, before % cuts, *pairs[before // cuts], peer(i), me).wait_send()
            across(kind, u, src, dst, peer(i), me).start()

        pltpu.make_async_copy(src.at[u, me], dst.at[u, me], lsem.at[kind, u]).start()

    def arrived(kind, u):
        src, dst = pairs[kind]

        @pl.loop(0, n - 1)
        def _(i):
            across(kind, u, src, dst, me, peer(i)).wait_recv()

        pltpu.make_async_copy(src.at[u, me], dst.at[u, me], lsem.at[kind, u]).wait()

    def left(kind, u):
        @pl.loop(0, n - 1)
        def _(i):
            across(kind, u, *pairs[kind], peer(i), me).wait_send()

    def beside(kind, src, dst, to, slot):
        return pltpu.make_async_remote_copy(
            src_ref=src, dst_ref=dst.at[slot],
            send_sem=dsend.at[kind, to], recv_sem=drecv.at[kind, slot],
            device_id={"dp": to, "seq": me}, device_id_type=pl.DeviceIdType.MESH,
        )

    def columns(u, body):
        @pl.loop(0, piece // tile)
        def _(t):
            start = pl.multiple_of(t * tile, tile)
            body(pl.ds(u * piece + start, tile), pl.ds(start, tile))

    def place(shape, row_dim):
        r = iota(shape, row_dim)
        rem = r & (chunk - 1)
        return (rem >> log2(offs)) * bs + (r >> log2(chunk)) * offs + (rem & (offs - 1))

    def to_chunks(parts, dst, u, cols):
        if offs % 8 == 0:
            for p in range(n):
                span = slice(p * offs, (p + 1) * offs)
                dst[u, p, :, cols] = jnp.concatenate([x[span] for x in parts], axis=0).astype(BF16)
        else:
            order = onehot(place((rows, rows), 0) == iota((rows, rows), 1))
            whole = jnp.concatenate(parts, axis=0).astype(BF16)
            dst[u, :, :, cols] = dot(order, whole).astype(BF16).reshape(n, chunk, tile)

    def from_chunks(src, u, cols):
        if offs % 8 == 0:
            pieces = [src[u, p, :, cols].astype(F32) for p in range(n)]
            return [
                jnp.concatenate([x[b * offs : (b + 1) * offs] for x in pieces], axis=0)
                for b in range(blocks)
            ]
        order = onehot(place((rows, rows), 1) == iota((rows, rows), 0))
        whole = dot(order, src[u, :, :, cols].reshape(rows, tile))
        return [whole[b * bs : (b + 1) * bs] for b in range(blocks)]

    for u in range(cuts):
        fetch(u, 0).wait()
        fetch(u, 1).wait()

        def gate(cols, at):
            parts = []
            for b in range(blocks):
                span = slice(b * bs, (b + 1) * bs)
                parts.append(c_ref[span, cols].astype(F32) * q_ref[span, cols].astype(F32))
            to_chunks(parts, gs, u, at)

        columns(u, gate)
        if u == 0:
            pl.semaphore_wait(barrier, n + ndp - 2)
        exchange(G, u)

    @pl.loop(0, ndp - 1)
    def _(i):
        beside(0, w_ref, wg, mate(i), core).start()
        beside(1, mx_ref, mg, mate(i), core).start()

    wg[core] = w_ref[...]
    mg[core] = mx_ref[...]

    @pl.loop(0, ndp - 1)
    def _(i):
        beside(0, w_ref, wg, core, mate(i)).wait_recv()
        beside(1, mx_ref, mg, core, mate(i)).wait_recv()

    for h in range(ndp):
        wfull[:, h * a_loc : (h + 1) * a_loc, :] = wg[h]

    for u in range(cuts):
        fetch(u, 2).wait()
        fetch(u, 3).wait()

        def first(cols, at):
            parts = []
            for b in range(blocks):
                span = slice(b * bs, (b + 1) * bs)
                x = (k_ref[span, cols].astype(F32) * v_ref[span, cols].astype(F32)).astype(BF16)
                prod[span, cols] = x
                parts.append(dot(wfull[b], x))
            to_chunks(parts, fs, u, at)

        columns(u, first)

    named = jnp.zeros((nb, nb), F32)
    index = bi_ref[...]
    for t in range(nnz):
        named = jnp.where(index[t : t + 1, :] == iota((nb, nb), 0), 1.0, named)
    named = named.astype(BF16)
    spread = onehot((iota((nb, rows), 1) >> log2(offs)) == iota((nb, rows), 0))
    same = ((iota((part, rows), 0) ^ iota((part, rows), 1)) & (offs - 1)) == 0
    r, c = iota((part, part), 0), iota((part, part), 1)
    by_block = onehot((r & (offs - 1)) * own + (r >> log2(offs)) == c)
    by_offset = onehot((c & (offs - 1)) * own + (c >> log2(offs)) == r)
    for h in range(ndp):
        span = slice(h * part, (h + 1) * part)
        lift = onehot((iota((part, nb), 0) >> log2(offs)) + h * own == iota((part, nb), 1))
        pattern = dot_nt(lift, named)
        pr[h] = pattern
        masked = (dot(by_block, mg[h]) * pattern).astype(BF16)
        bmat[span, :] = jnp.where(same, dot(masked, spread), 0.0).astype(BF16)
    btm[...] = bmat[...].T

    for u in range(cuts):
        exchange(F, u)

    def second(matrix, kind, u, back):
        src, dst = pairs[kind][1], pairs[back][0]
        arrived(kind, u)

        def body(cols, at):
            x = src[u, :, :, at].reshape(rows, tile)
            dst[u, :, :, at] = dot(matrix[...], x).astype(BF16).reshape(n, chunk, tile)

        columns(u, body)
        exchange(back, u)

    for u in range(cuts):
        second(btm, G, u, H)
    for u in range(cuts):
        second(bmat, F, u, M)

    step = part // chunk
    for h in range(ndp):
        span = slice(h * step, (h + 1) * step)
        terms = sum(
            dot_nt(gr[u, span].reshape(part, piece), fr[u].reshape(rows, piece))
            for u in range(cuts)
        )
        terms = jnp.where(same, terms, 0.0)
        kept = sum(dot_nt(x, spread) for x in thirds(terms))
        gms[h] = kept * pr[h]

    @pl.loop(0, ndp - 1)
    def _(i):
        beside(2, gms.at[mate(i)], gmr, mate(i), core).start()

    for u in range(cuts):
        arrived(H, u)

        def grad_inputs(cols, at):
            parts = from_chunks(hr, u, at)
            for b in range(blocks):
                span = slice(b * bs, (b + 1) * bs)
                x = parts[b].astype(BF16)
                gfn[span, cols] = x
                gp = dot_tn(wfull[b], x)
                gk_ref[span, cols] = (gp * v_ref[span, cols].astype(F32)).astype(BF16)
                gv_ref[span, cols] = (gp * k_ref[span, cols].astype(F32)).astype(BF16)

        columns(u, grad_inputs)

    for b in range(blocks):
        span = slice(b * bs, (b + 1) * bs)
        terms = dot_nt(gfn[span, :], prod[span, :])
        for h in range(ndp):
            gbs[h, b] = terms[h * a_loc : (h + 1) * a_loc]

    @pl.loop(0, ndp - 1)
    def _(i):
        beside(3, gbs.at[mate(i)], gbr, mate(i), core).start()

    gmr[core] = gms[core]
    gbr[core] = gbs[core]

    @pl.loop(0, ndp - 1)
    def _(i):
        beside(2, gms.at[mate(i)], gmr, core, mate(i)).wait_recv()
        beside(3, gbs.at[mate(i)], gbr, core, mate(i)).wait_recv()

    gb_ref[...] = sum(gbr[h] for h in range(ndp))
    total = sum(gmr[h] for h in range(ndp))
    gm_ref[...] = sum(dot(by_offset, x) for x in thirds(total))

    @pl.loop(0, ndp - 1)
    def _(i):
        beside(0, w_ref, wg, mate(i), core).wait_send()
        beside(1, mx_ref, mg, mate(i), core).wait_send()
        beside(2, gms.at[mate(i)], gmr, mate(i), core).wait_send()
        beside(3, gbs.at[mate(i)], gbr, mate(i), core).wait_send()

    for u in range(cuts):
        arrived(M, u)

        def outputs(cols, at):
            parts = from_chunks(mr, u, at)
            for b in range(blocks):
                span = slice(b * bs, (b + 1) * bs)
                o_ref[span, cols] = (q_ref[span, cols].astype(F32) * parts[b]).astype(BF16)
                gq_ref[span, cols] = (c_ref[span, cols].astype(F32) * parts[b]).astype(BF16)

        columns(u, outputs)

    for last in range(4 * cuts - depth, 4 * cuts):
        left(last // cuts, last % cuts)


def write_out(*refs):
    count = len(refs) // 2
    sems = refs[-1]
    copies = [
        pltpu.make_async_copy(refs[i], refs[count + i], sems.at[i]) for i in range(count)
    ]
    for copy in copies:
        copy.start()
    for copy in copies:
        copy.wait()


def on_device(n, ndp, query, key, value, block_weights, mix_weights, block_index, cotangent):
    _, rows, width = query.shape
    nb = block_index.shape[0]
    blocks, a_loc, bs = block_weights.shape
    offs, own, _ = mix_weights.shape
    chunk, part = blocks * offs, own * offs
    vmem = pl.BlockSpec(memory_space=pltpu.VMEM)
    anywhere = pl.BlockSpec(memory_space=pl.ANY)
    cuts = 2
    moved = pltpu.VMEM((cuts, n, chunk, width // cuts), BF16)
    shapes = [((rows, width), BF16)] * 4 + [((blocks, a_loc, bs), F32), ((offs * own, nb), F32)]
    dma = pltpu.SemaphoreType.DMA
    outs = pl.pallas_call(
        functools.partial(kernel, n, ndp, cuts, 256),
        out_shape=tuple(pltpu.VMEM(*shape) for shape in shapes),
        in_specs=[anywhere] * 4 + [vmem] * 3,
        out_specs=(vmem,) * 6,
        scratch_shapes=[moved] * 8 + [
            pltpu.VMEM((rows, width), BF16),
            pltpu.VMEM((rows, width), BF16),
            pltpu.VMEM((rows, rows), BF16),
            pltpu.VMEM((rows, rows), BF16),
            pltpu.VMEM((blocks, bs, bs), BF16),
            pltpu.VMEM((ndp, blocks, a_loc, bs), BF16),
            pltpu.VMEM((ndp, offs * own, nb), BF16),
            pltpu.VMEM((ndp, part, nb), F32),
            pltpu.VMEM((ndp, part, nb), F32),
            pltpu.VMEM((ndp, part, nb), F32),
            pltpu.VMEM((ndp, blocks, a_loc, bs), F32),
            pltpu.VMEM((ndp, blocks, a_loc, bs), F32),
            *[pltpu.VMEM((rows, width), BF16)] * 4,
            dma((4, cuts, n)), dma((4, cuts, n)), dma((4, ndp)), dma((4, ndp)),
            dma((4, cuts)), dma((cuts, 4)),
        ],
        compiler_params=pltpu.CompilerParams(
            collective_id=0, has_side_effects=True, vmem_limit_bytes=48 * 1024 * 1024
        ),
        cost_estimate=pl.CostEstimate(
            flops=7 * 2 * rows * rows * width, bytes_accessed=16 * rows * width, transcendentals=0
        ),
        name="monarch",
    )(
        query[0], key[0], value[0], cotangent[0],
        block_weights, mix_weights.reshape(offs * own, nb), block_index.T,
    )
    outs = pl.pallas_call(
        write_out,
        out_shape=tuple(jax.ShapeDtypeStruct(*shape) for shape in shapes),
        in_specs=[vmem] * 6,
        out_specs=(anywhere,) * 6,
        scratch_shapes=[dma((6,))],
        compiler_params=pltpu.CompilerParams(vmem_limit_bytes=8 * 1024 * 1024),
        name="write_out",
    )(*outs)
    output, grad_query, grad_key, grad_value, grad_blocks, grad_mix = outs
    return (
        output[None], grad_query[None], grad_key[None], grad_value[None],
        grad_blocks, grad_mix.reshape(offs, own, nb),
    )


def solution(mesh):
    wide, split = P("dp", "seq", None), P("seq", "dp", None)
    return jax.shard_map(
        functools.partial(on_device, mesh.shape["seq"], mesh.shape["dp"]),
        mesh=mesh,
        in_specs=(wide, wide, wide, split, split, P(), wide),
        out_specs=(wide, wide, wide, wide, split, split),
        check_vma=False,
    )
```
